512 devices in a mesh: sub: 16 (over z_lo, x), row: 32 (over y, z_hi, core).
Axes of the slice: x: 4, y: 8, z: 8 (z_hi: 2, z_lo: 4; z = z_hi * 4 + z_lo), core: 2. Of those that a mesh axis runs over, the one named last changes fastest.
Arguments:
- phi_rows: bfloat16 [524288, 400], P(('sub', 'row')), may hold values from -0.125 to 0.125
- psi_rows: bfloat16 [524288, 1536], P(('sub', 'row')), may hold values from -0.125 to 0.125
- stiffness: bfloat16 [4096, 128, 128], P(('sub', 'row')), may hold values from -0.046875 to 0.046875
- coord_fixed: bfloat16 [16, 256, 400], P('sub', 'row'), may hold values from -6 to 6
- coord_con: bfloat16 [16, 256, 1536], P('sub', 'row'), may hold values from -6 to 6
- elem_zone: int32 [4096], P(('sub', 'row')), may hold values from 0 to 1023
- partner: int32 [4096], P(('sub', 'row')), may hold values from 0 to 7, as said below
- owner_slot: int32 [1024], replicated, may hold values from 0 to 1023, each once
Outputs:
- zone_sens: float32 [1024, 256], P(('sub', 'row'))
The draws below stay inside these ranges and needn't reach their ends.
Inputs may be any that keep to these rules, and one draw needn't show every extreme that they name: partner[b] differs from b % 8.
All inputs are finite; a program needn't handle non-finite values.
Results may differ from the reference program's by a relative error of at most 0.015.
Values may be sent and summed in bfloat16 or wider, within the bound.
No kernel may reach another device: no remote copies, remote signals or barrier semaphores. Data moves between devices by JAX's collectives and lax.ppermute only.
A program may use at most 64 MiB of HBM per device.

```python
import jax
import jax.numpy as jnp
from jax import lax

NF = 400
NC = 1536
MODES = 256
BLOCK = 128
BLK_DEV = 8
ROWS = 524288
NBLK = 4096
ZONES = 1024
N_SUB = 16


def draw_partner(key, part):
    key = jax.random.fold_in(key, 11)
    within = jnp.arange(NBLK, dtype=jnp.int32) % BLK_DEV
    offset = jax.random.randint(key, (NBLK,), 1, BLK_DEV, dtype=jnp.int32)
    return ((within + offset) % BLK_DEV).astype(jnp.int32)


def with_ends(drawn, own_key, low, largest):
    longest = drawn.shape.index(max(drawn.shape))
    spots = []
    for shift in (0, 1):
        where = [jax.random.randint(jax.random.fold_in(own_key, axis), (), 0, length) for axis, length in enumerate(drawn.shape)]
        where[longest] = (where[longest] + shift) % drawn.shape[longest]
        spots.append(tuple(where))
    return drawn.at[spots[0]].set(low).at[spots[1]].set(largest)


def level_of(stream_key, shape, split, least, largest):
    def one(axis_at, shards_of):
        draws = jax.random.uniform(jax.random.fold_in(jax.random.fold_in(stream_key, 6), axis_at), (shards_of,), jnp.float32, least / len(split), largest / len(split))
        return jnp.repeat(jnp.exp(draws), shape[axis_at] // shards_of).reshape((-1,) + (1,) * (len(shape) - axis_at - 1))

    gain = one(*split[0])
    for cut in split[1:]:
        gain = gain * one(*cut)
    return gain


def normal_values(rng, extent, width, bound, pieces=(), kind=jnp.bfloat16):
    gain = level_of(rng, extent, pieces, -0.22, 0.18) if pieces else 1.0
    drawn = jax.random.normal(rng, extent, jnp.float32) * width * gain
    return jnp.minimum(jnp.maximum(drawn, -bound), bound).astype(kind)


def setup_inputs(seed: int = 0) -> dict:
    seeds = jax.random.split(jax.random.key(seed), 9)
    phi_rows = normal_values(seeds[0], (ROWS, NF), (NF + NC) ** -0.5, 0.125, ((0, 512),))
    psi_rows = normal_values(seeds[1], (ROWS, NC), (NF + NC) ** -0.5, 0.125, ((0, 512),))
    stiffness = normal_values(seeds[2], (NBLK, BLOCK, BLOCK), (BLOCK * BLOCK) ** -0.5, 0.046875, ((0, 512),))
    coord_fixed = normal_values(seeds[3], (N_SUB, MODES, NF), 1.0, 6.0, ((0, 16), (1, 32)))
    coord_con = normal_values(seeds[4], (N_SUB, MODES, NC), 1.0, 6.0, ((0, 16), (1, 32)))
    elem_zone = with_ends(jax.random.randint(seeds[5], (NBLK,), 0, ZONES), jax.random.fold_in(seeds[5], 1), 0, ZONES - 1).astype(jnp.int32)
    partner = draw_partner(jax.random.fold_in(seeds[8], 71), 0)
    owner_slot = jax.random.permutation(seeds[7], ZONES).astype(jnp.int32)
    return dict(phi_rows=phi_rows, psi_rows=psi_rows, stiffness=stiffness, coord_fixed=coord_fixed, coord_con=coord_con, elem_zone=elem_zone, partner=partner, owner_slot=owner_slot)


def group_energy(items):
    phi, psi, qf, qc, stiff, part = items
    dims = (((1,), (1,)), ((), ()))
    shapes = (lax.dot_general(phi, qf, dims, preferred_element_type=jnp.float32)
              + lax.dot_general(psi, qc, dims, preferred_element_type=jnp.float32)).astype(jnp.bfloat16)
    blocks = shapes.reshape(-1, BLOCK, MODES)
    count = blocks.shape[0]
    base = (jnp.arange(count, dtype=jnp.int32) // BLK_DEV) * BLK_DEV
    other = blocks[(base + part).astype(jnp.int32)]
    relative = (blocks.astype(jnp.float32) - other.astype(jnp.float32)).astype(jnp.bfloat16)
    rel32 = relative.astype(jnp.float32)
    pushed = jnp.einsum("bij,bjm->bim", stiff.astype(jnp.float32), rel32, precision=lax.Precision.HIGHEST)
    return jnp.sum(rel32 * pushed, axis=1)


def reference(phi_rows, psi_rows, stiffness, coord_fixed, coord_con, elem_zone, partner, owner_slot):
    nsub = coord_fixed.shape[0]
    energy = lax.map(group_energy, (phi_rows.reshape(nsub, -1, NF), psi_rows.reshape(nsub, -1, NC),
                                    coord_fixed, coord_con,
                                    stiffness.reshape(nsub, -1, BLOCK, BLOCK), partner.reshape(nsub, -1)))
    slots = owner_slot[elem_zone].astype(jnp.int32)
    return jax.ops.segment_sum(energy.reshape(-1, MODES), slots, ZONES)
```

```python
import jax
import jax.numpy as jnp
from jax import lax
from jax.experimental import pallas as pl
from jax.experimental.pallas import tpu as pltpu
from jax.sharding import Mesh, PartitionSpec as P

AXES = ("zlo", "x", "y", "zhi", "core")
SIZES = (4, 4, 8, 2, 2)
ROW = ("y", "zhi", "core")
REST = ("zlo", "x", "zhi", "core")
NT = (((1,), (1,)), ((), ()))


def energy_kernel(partner_ref, shapes_ref, stiffness_ref, out_ref):
    nblocks = shapes_ref.shape[0]
    rows = []
    for b in range(nblocks):
        own = shapes_ref[b].astype(jnp.float32)
        other = shapes_ref[partner_ref[b]].astype(jnp.float32)
        relative = (own - other).astype(jnp.bfloat16)
        pushed = jnp.dot(stiffness_ref[b], relative, preferred_element_type=jnp.float32)
        rows.append(jnp.sum(relative.astype(jnp.float32) * pushed, axis=0, keepdims=True))
    energy = jnp.concatenate(rows, axis=0).astype(jnp.bfloat16)
    for i in range(out_ref.shape[0]):
        out_ref[i] = energy


def block_energy(partner, shapes, stiffness, copies):
    nblocks, _, modes = shapes.shape
    vmem = pl.BlockSpec(memory_space=pltpu.VMEM)
    return pl.pallas_call(
        energy_kernel,
        out_shape=jax.ShapeDtypeStruct((copies, nblocks, modes), jnp.bfloat16),
        in_specs=[pl.BlockSpec(memory_space=pltpu.SMEM), vmem, vmem],
        out_specs=vmem,
        compiler_params=pltpu.CompilerParams(vmem_limit_bytes=16 * 2**20),
        cost_estimate=pl.CostEstimate(flops=2 * nblocks * 128 * 128 * modes, bytes_accessed=2**20, transcendentals=0),
    )(partner, shapes, stiffness)


def on_device(
    phi_rows, psi_rows, stiffness, coord_fixed, coord_con, elem_zone, partner, owner_slot
):
    nblocks, block, _ = stiffness.shape
    nf, nc = coord_fixed.shape[2], coord_con.shape[2]
    mine = coord_fixed.shape[1]
    zones = owner_slot.shape[0]
    n_row = 32
    modes = n_row * mine

    hits = elem_zone[:, None] == jnp.arange(zones, dtype=jnp.int32)[None, :]
    slots = jnp.sum(jnp.where(hits, owner_slot[None, :], 0), axis=1)
    coded = jnp.stack([slots // 32, slots % 32], axis=1).astype(jnp.bfloat16)
    pad = -(nc + nf + 2) % 128
    packet = jnp.concatenate(
        [coord_con[0], coord_fixed[0], coded, jnp.zeros((mine, pad), jnp.bfloat16)], axis=1
    )
    gathered = lax.all_to_all(
        jnp.broadcast_to(packet[None], (n_row, *packet.shape)), ROW, 0, 0, tiled=True
    )
    coords = gathered.reshape(modes, -1)

    total = lax.dot_general(psi_rows, coords[:, :nc], NT, preferred_element_type=jnp.float32)
    total = total + lax.dot_general(
        phi_rows, coords[:, nc : nc + nf], NT, preferred_element_type=jnp.float32
    )
    shapes = total.astype(jnp.bfloat16).reshape(nblocks, block, modes)
    n_y = 8
    energy = block_energy(partner, shapes, stiffness, n_y)

    along_y = lax.all_to_all(energy, "y", 0, 0, tiled=True).reshape(n_y * nblocks, modes)
    kept = gathered[:, :, nc + nf : nc + nf + 2].reshape(n_y, 4, nblocks, 2).astype(jnp.int32)
    at = lax.axis_index("zhi") * 2 + lax.axis_index("core")
    kept = lax.dynamic_index_in_dim(kept, at, axis=1, keepdims=False)
    block_slots = (kept[:, :, 0] * 32 + kept[:, :, 1]).reshape(n_y * nblocks)
    n_rest = 64
    dest = jnp.arange(2 * n_rest, dtype=jnp.int32)
    peer = dest // 2
    owned = 2 * ((peer // 4) * n_row + lax.axis_index("y") * 4 + peer % 4) + dest % 2
    chosen = (owned[:, None] == block_slots[None, :]).astype(jnp.bfloat16)
    partial_sums = jnp.dot(chosen, along_y, preferred_element_type=jnp.float32)
    partial_sums = partial_sums.astype(jnp.bfloat16).reshape(n_rest, 2, modes)
    received = lax.all_to_all(partial_sums, REST, 0, 0, tiled=True)
    return jnp.sum(received.astype(jnp.float32), axis=0)


def solution(mesh):
    fine = Mesh(mesh.devices.reshape(SIZES), AXES)
    sub, row = AXES[:2], AXES[2:]
    placed = (
        P(AXES, None),
        P(AXES, None),
        P(AXES, None, None),
        P(sub, row, None),
        P(sub, row, None),
        P(AXES),
        P(AXES),
        P(),
    )
    return jax.shard_map(
        on_device, mesh=fine, in_specs=placed, out_specs=P(AXES, None), check_vma=False
    )
```

```python
import jax
import jax.numpy as jnp
from jax import lax
from jax.experimental import pallas as pl
from jax.experimental.pallas import tpu as pltpu
from jax.sharding import Mesh, PartitionSpec as P

AXES = ("zlo", "x", "y", "zhi", "core")
SIZES = (4, 4, 8, 2, 2)
N_ROW = 32
NT = (((1,), (1,)), ((), ()))
TN = (((0,), (0,)), ((), ()))
VMEM = pl.BlockSpec(memory_space=pltpu.VMEM)
SMEM = pl.BlockSpec(memory_space=pltpu.SMEM)
CODE_LANES = 128


def packet_kernel(con_ref, fixed_ref, out_ref):
    mine, nf = fixed_ref.shape
    nc = con_ref.shape[1]
    whole = nf // 128 * 128
    head = jnp.concatenate([con_ref[...], fixed_ref[:, :whole]], axis=1)
    blank = jnp.zeros((mine, out_ref.shape[2] - nc - nf), out_ref.dtype)
    tail = jnp.concatenate([fixed_ref[:, whole:], blank], axis=1)
    for i in range(out_ref.shape[0]):
        out_ref[i, :, : nc + whole] = head
        out_ref[i, :, nc + whole :] = tail


def packets(con, fixed, copies, width):
    return pl.pallas_call(
        packet_kernel,
        out_shape=jax.ShapeDtypeStruct((copies, con.shape[0], width), con.dtype),
        in_specs=[VMEM, VMEM],
        out_specs=VMEM,
        compiler_params=pltpu.CompilerParams(vmem_limit_bytes=56 * 2**20),
    )(con, fixed)


def early_kernel(elem_zone_ref, owner_slot_ref, phi_ref, rows_ref, codes_ref):
    nf, rows = phi_ref.shape
    rows_ref[:, :nf] = phi_ref[...].T
    rows_ref[:, nf:] = jnp.zeros((rows, rows_ref.shape[1] - nf), rows_ref.dtype)
    row = lax.broadcasted_iota(jnp.int32, codes_ref.shape, 0)
    lane = lax.broadcasted_iota(jnp.int32, codes_ref.shape, 1)
    codes = jnp.zeros(codes_ref.shape, jnp.int32)
    for b in range(codes_ref.shape[0]):
        slot = owner_slot_ref[elem_zone_ref[b]]
        codes = jnp.where((row == b) & (lane == 0), slot // 32, codes)
        codes = jnp.where((row == b) & (lane == 1), slot % 32, codes)
    codes_ref[...] = codes.astype(jnp.float32).astype(codes_ref.dtype)


def early(elem_zone, owner_slot, phi_t, width):
    return pl.pallas_call(
        early_kernel,
        out_shape=(
            jax.ShapeDtypeStruct((phi_t.shape[1], width), phi_t.dtype),
            jax.ShapeDtypeStruct((elem_zone.shape[0], CODE_LANES), jnp.bfloat16),
        ),
        in_specs=[SMEM, SMEM, VMEM],
        out_specs=(VMEM, VMEM),
        compiler_params=pltpu.CompilerParams(vmem_limit_bytes=16 * 2**20),
        cost_estimate=pl.CostEstimate(flops=0, bytes_accessed=8 * 2**20, transcendentals=0),
    )(elem_zone, owner_slot, phi_t)


def own_shapes_kernel(own_ref, phi_ref, psi_ref, shapes_ref, kept_ref, arrived):
    rows, nc = psi_ref.shape
    chunks = arrived.shape[0]
    step = rows // chunks
    parts = [pl.ds(i * step, step) for i in range(chunks)]
    copies = [
        pltpu.make_async_copy(psi_ref.at[part], kept_ref.at[part], arrived.at[i])
        for i, part in enumerate(parts)
    ]
    for copy in copies:
        copy.start()
    for part, copy in zip(parts, copies):
        total = lax.dot_general(
            phi_ref[part], own_ref[:, nc:], NT, preferred_element_type=jnp.float32
        )
        copy.wait()
        total = total + lax.dot_general(
            kept_ref[part], own_ref[:, :nc], NT, preferred_element_type=jnp.float32
        )
        shapes_ref[part] = total.astype(shapes_ref.dtype)


def own_shapes(own, phi, psi, chunks=4):
    rows, nc = psi.shape
    return pl.pallas_call(
        own_shapes_kernel,
        out_shape=(
            pltpu.VMEM((rows, own.shape[0]), jnp.bfloat16),
            pltpu.VMEM((rows, nc), psi.dtype),
        ),
        in_specs=[VMEM, VMEM, pl.BlockSpec(memory_space=pltpu.HBM)],
        out_specs=(VMEM, VMEM),
        scratch_shapes=[pltpu.SemaphoreType.DMA((chunks,))],
        compiler_params=pltpu.CompilerParams(vmem_limit_bytes=52 * 2**20),
        cost_estimate=pl.CostEstimate(flops=2**29, bytes_accessed=5 * 2**20, transcendentals=0),
    )(own, phi, psi)


def energy_kernel(
    partner_ref, other_ref, phi_ref, psi_ref, own_shapes_ref, stiffness_ref, codes_ref, out_ref, shapes
):
    half = other_ref.shape[0]
    nc = psi_ref.shape[1]
    nblocks, block, _ = stiffness_ref.shape
    modes = 2 * half
    total = lax.dot_general(phi_ref[...], other_ref[:, nc:], NT, preferred_element_type=jnp.float32)
    total = total + lax.dot_general(
        psi_ref[...], other_ref[:, :nc], NT, preferred_element_type=jnp.float32
    )
    for b in range(nblocks):
        part = slice(b * block, (b + 1) * block)
        shapes[b, :, :half] = own_shapes_ref[part]
        shapes[b, :, half:] = total[part].astype(shapes.dtype)
    sums = []
    for b in range(nblocks):
        own = shapes[b].astype(jnp.float32)
        partner = shapes[partner_ref[b]].astype(jnp.float32)
        relative = (own - partner).astype(jnp.bfloat16)
        pushed = jnp.dot(stiffness_ref[b], relative, preferred_element_type=jnp.float32)
        sums.append(jnp.sum(relative.astype(jnp.float32) * pushed, axis=0, keepdims=True))
    energy = jnp.concatenate(sums, axis=0).astype(jnp.bfloat16)
    source = lax.broadcasted_iota(jnp.int32, (modes, modes), 0)
    target = lax.broadcasted_iota(jnp.int32, (modes, modes), 1)
    core = (source // half + lax.axis_index("core")) % 2
    ordered = (source % half) // 8 * 16 + core * 8 + source % 8
    move = (ordered == target).astype(jnp.float32).astype(jnp.bfloat16)
    energy = jnp.dot(energy, move, preferred_element_type=jnp.float32).astype(jnp.bfloat16)
    for i in range(out_ref.shape[0]):
        out_ref[i, :, :modes] = energy
        out_ref[i, :, modes:] = codes_ref[...]


def block_energy(partner, other, phi, psi, shapes, stiffness, codes, copies):
    nblocks, block, _ = stiffness.shape
    modes = 2 * other.shape[0]
    return pl.pallas_call(
        energy_kernel,
        out_shape=jax.ShapeDtypeStruct((copies, nblocks, modes + CODE_LANES), jnp.bfloat16),
        in_specs=[SMEM, VMEM, VMEM, VMEM, VMEM, VMEM, VMEM],
        out_specs=VMEM,
        scratch_shapes=[pltpu.VMEM((nblocks, block, modes), jnp.bfloat16)],
        compiler_params=pltpu.CompilerParams(vmem_limit_bytes=24 * 2**20),
        cost_estimate=pl.CostEstimate(flops=2**30, bytes_accessed=6 * 2**20, transcendentals=0),
    )(partner, other, phi, psi, shapes, stiffness, codes)


def zone_kernel(packet_ref, out_ref):
    peers, nblocks, width = packet_ref.shape
    modes = width - CODE_LANES
    packet = packet_ref[...].astype(jnp.float32).reshape(peers * nblocks, width)
    slot = packet[:, modes : modes + 1] * 32.0 + packet[:, modes + 1 : modes + 2]
    place = lax.broadcasted_iota(jnp.int32, (1, out_ref.shape[0]), 1)
    corner = lax.axis_index("zlo") * 256 + lax.axis_index("zhi") * 4 + lax.axis_index("core") * 2
    owned = (corner + place // 2 * 8 + place % 2).astype(jnp.float32)
    chosen = (slot == owned).astype(jnp.float32).astype(jnp.bfloat16)
    energy = packet[:, :modes].astype(jnp.bfloat16)
    sums = lax.dot_general(chosen, energy, TN, preferred_element_type=jnp.float32)
    out_ref[...] = sums.astype(out_ref.dtype)


def zone_sums(packet, slots):
    return pl.pallas_call(
        zone_kernel,
        out_shape=jax.ShapeDtypeStruct((slots, packet.shape[2] - CODE_LANES), jnp.bfloat16),
        in_specs=[VMEM],
        out_specs=VMEM,
        compiler_params=pltpu.CompilerParams(vmem_limit_bytes=8 * 2**20),
    )(packet)


def on_device(
    phi_rows, psi_rows, stiffness, coord_fixed, coord_con, elem_zone, partner, owner_slot
):
    nf, nc = coord_fixed.shape[2], coord_con.shape[2]
    mine = coord_fixed.shape[1]
    modes = N_ROW * mine
    width = nc + nf + -(nc + nf) % 128

    sent = packets(coord_con[0], coord_fixed[0], N_ROW // 2, width)
    own = lax.all_to_all(sent, ("y", "zhi"), 0, 0, tiled=True).reshape(modes // 2, width)

    phi, codes = early(elem_zone, owner_slot, phi_rows.T, width - nc)
    own, phi, codes = lax.optimization_barrier((own, phi, codes))
    other = lax.ppermute(own, "core", [(0, 1), (1, 0)])

    shapes, psi = own_shapes(own, phi, psi_rows)
    energy = block_energy(partner, other, phi, psi, shapes, stiffness, codes, 16)
    along_z = lax.all_to_all(energy, ("zlo", "zhi", "core"), 0, 0, tiled=True)
    partial_sums = zone_sums(along_z, 64).reshape(32, 2, modes)
    received = lax.all_to_all(partial_sums, ("x", "y"), 0, 0, tiled=True)
    return jnp.sum(received.astype(jnp.float32), axis=0)


def solution(mesh):
    fine = Mesh(mesh.devices.reshape(SIZES), AXES)
    sub, row = AXES[:2], AXES[2:]
    placed = (
        P(AXES, None),
        P(AXES, None),
        P(AXES, None, None),
        P(sub, row, None),
        P(sub, row, None),
        P(AXES),
        P(AXES),
        P(),
    )
    return jax.shard_map(
        on_device, mesh=fine, in_specs=placed, out_specs=P(AXES, None), check_vma=False
    )
```

```python
import jax
import jax.numpy as jnp
from jax import lax
from jax.experimental import pallas as pl
from jax.experimental.pallas import tpu as pltpu
from jax.sharding import Mesh, PartitionSpec as P

AXES = ("zlo", "x", "y", "zhi", "core")
SIZES = (4, 4, 8, 2, 2)
SIZE = dict(zip(AXES, SIZES))
SLOT_STEP = {"zlo": 256, "x": 64, "y": 8, "zhi": 4, "core": 2}
FIRST = ("x", "core")
SECOND = ("zlo", "y", "zhi")
N_FIRST = 8
N_SECOND = 64
N_ROW = 32
NT = (((1,), (1,)), ((), ()))
TN = (((0,), (0,)), ((), ()))
VMEM = pl.BlockSpec(memory_space=pltpu.VMEM)
SMEM = pl.BlockSpec(memory_space=pltpu.SMEM)
CODE_LANES = 128


def packet_kernel(con_ref, fixed_ref, out_ref):
    mine, nf = fixed_ref.shape
    nc = con_ref.shape[1]
    whole = nf // 128 * 128
    head = jnp.concatenate([con_ref[...], fixed_ref[:, :whole]], axis=1)
    blank = jnp.zeros((mine, out_ref.shape[2] - nc - nf), out_ref.dtype)
    tail = jnp.concatenate([fixed_ref[:, whole:], blank], axis=1)
    for i in range(out_ref.shape[0]):
        out_ref[i, :, : nc + whole] = head
        out_ref[i, :, nc + whole :] = tail


def packets(con, fixed, copies, width):
    return pl.pallas_call(
        packet_kernel,
        out_shape=jax.ShapeDtypeStruct((copies, con.shape[0], width), con.dtype),
        in_specs=[VMEM, VMEM],
        out_specs=VMEM,
        compiler_params=pltpu.CompilerParams(vmem_limit_bytes=56 * 2**20),
    )(con, fixed)


def early_kernel(elem_zone_ref, owner_slot_ref, phi_ref, rows_ref, codes_ref):
    nf, rows = phi_ref.shape
    rows_ref[:, :nf] = phi_ref[...].T
    rows_ref[:, nf:] = jnp.zeros((rows, rows_ref.shape[1] - nf), rows_ref.dtype)
    row = lax.broadcasted_iota(jnp.int32, codes_ref.shape, 0)
    lane = lax.broadcasted_iota(jnp.int32, codes_ref.shape, 1)
    codes = jnp.zeros(codes_ref.shape, jnp.int32)
    for b in range(codes_ref.shape[0]):
        slot = owner_slot_ref[elem_zone_ref[b]]
        codes = jnp.where((row == b) & (lane == 0), slot // 32, codes)
        codes = jnp.where((row == b) & (lane == 1), slot % 32, codes)
    codes_ref[...] = codes.astype(jnp.float32).astype(codes_ref.dtype)


def early(elem_zone, owner_slot, phi_t, width):
    return pl.pallas_call(
        early_kernel,
        out_shape=(
            jax.ShapeDtypeStruct((phi_t.shape[1], width), phi_t.dtype),
            jax.ShapeDtypeStruct((elem_zone.shape[0], CODE_LANES), jnp.bfloat16),
        ),
        in_specs=[SMEM, SMEM, VMEM],
        out_specs=(VMEM, VMEM),
        compiler_params=pltpu.CompilerParams(vmem_limit_bytes=16 * 2**20),
        cost_estimate=pl.CostEstimate(flops=0, bytes_accessed=8 * 2**20, transcendentals=0),
    )(elem_zone, owner_slot, phi_t)


def fetch_kernel(psi_ref, kept_ref, arrived):
    chunks = arrived.shape[0]
    step = psi_ref.shape[0] // chunks
    parts = [pl.ds(i * step, step) for i in range(chunks)]
    copies = [
        pltpu.make_async_copy(psi_ref.at[part], kept_ref.at[part], arrived.at[i])
        for i, part in enumerate(parts)
    ]
    for copy in copies:
        copy.start()
    for copy in copies:
        copy.wait()


def fetched(psi, chunks=4):
    return pl.pallas_call(
        fetch_kernel,
        out_shape=pltpu.VMEM(psi.shape, psi.dtype),
        in_specs=[pl.BlockSpec(memory_space=pltpu.HBM)],
        out_specs=VMEM,
        scratch_shapes=[pltpu.SemaphoreType.DMA((chunks,))],
        compiler_params=pltpu.CompilerParams(vmem_limit_bytes=57 * 2**20),
        cost_estimate=pl.CostEstimate(flops=0, bytes_accessed=6 * 2**20, transcendentals=0),
    )(psi)


def energy_kernel(
    partner_ref, own_ref, other_ref, phi_ref, psi_ref, stiffness_ref, codes_ref, out_ref, coords, shapes
):
    half = other_ref.shape[0]
    nc = psi_ref.shape[1]
    nblocks, block, _ = stiffness_ref.shape
    modes = 2 * half
    coords[:half] = own_ref[...]
    coords[half:] = other_ref[...]
    total = lax.dot_general(psi_ref[...], coords[:, :nc], NT, preferred_element_type=jnp.float32)
    total = total + lax.dot_general(
        phi_ref[...], coords[:, nc:], NT, preferred_element_type=jnp.float32
    )
    for b in range(nblocks):
        shapes[b] = total[b * block : (b + 1) * block].astype(shapes.dtype)
    sums = []
    for b in range(nblocks):
        own = shapes[b].astype(jnp.float32)
        partner = shapes[partner_ref[b]].astype(jnp.float32)
        relative = (own - partner).astype(jnp.bfloat16)
        pushed = jnp.dot(stiffness_ref[b], relative, preferred_element_type=jnp.float32)
        sums.append(jnp.sum(relative.astype(jnp.float32) * pushed, axis=0, keepdims=True))
    energy = jnp.concatenate(sums, axis=0).astype(jnp.bfloat16)
    source = lax.broadcasted_iota(jnp.int32, (modes, modes), 0)
    target = lax.broadcasted_iota(jnp.int32, (modes, modes), 1)
    core = (source // half + lax.axis_index("core")) % 2
    ordered = (source % half) // 8 * 16 + core * 8 + source % 8
    move = (ordered == target).astype(jnp.float32).astype(jnp.bfloat16)
    energy = jnp.dot(energy, move, preferred_element_type=jnp.float32).astype(jnp.bfloat16)
    for i in range(out_ref.shape[0]):
        out_ref[i, :, :modes] = energy
        out_ref[i, :, modes:] = codes_ref[...]


def block_energy(partner, own, other, phi, psi, stiffness, codes, copies):
    nblocks, block, _ = stiffness.shape
    modes = 2 * other.shape[0]
    return pl.pallas_call(
        energy_kernel,
        out_shape=jax.ShapeDtypeStruct((copies, nblocks, modes + CODE_LANES), jnp.bfloat16),
        in_specs=[SMEM, VMEM, VMEM, VMEM, VMEM, VMEM, VMEM],
        out_specs=VMEM,
        scratch_shapes=[
            pltpu.VMEM((modes, own.shape[1]), jnp.bfloat16),
            pltpu.VMEM((nblocks, block, modes), jnp.bfloat16),
        ],
        compiler_params=pltpu.CompilerParams(vmem_limit_bytes=24 * 2**20),
        cost_estimate=pl.CostEstimate(flops=2**30, bytes_accessed=6 * 2**20, transcendentals=0),
    )(partner, own, other, phi, psi, stiffness, codes)


def zone_kernel(packet_ref, out_ref):
    peers, nblocks, width = packet_ref.shape
    modes = width - CODE_LANES
    packet = packet_ref[...].astype(jnp.float32).reshape(peers * nblocks, width)
    slot = packet[:, modes : modes + 1] * 32.0 + packet[:, modes + 1 : modes + 2]
    place = lax.broadcasted_iota(jnp.int32, (1, out_ref.shape[0]), 1)
    owned = place % 2 + sum(SLOT_STEP[axis] * lax.axis_index(axis) for axis in FIRST)
    peer = place // 2
    for axis in reversed(SECOND):
        owned = owned + peer % SIZE[axis] * SLOT_STEP[axis]
        peer = peer // SIZE[axis]
    chosen = (slot == owned.astype(jnp.float32)).astype(jnp.float32).astype(jnp.bfloat16)
    energy = packet[:, :modes].astype(jnp.bfloat16)
    sums = lax.dot_general(chosen, energy, TN, preferred_element_type=jnp.float32)
    out_ref[...] = sums.astype(out_ref.dtype)


def zone_sums(packet, slots):
    return pl.pallas_call(
        zone_kernel,
        out_shape=jax.ShapeDtypeStruct((slots, packet.shape[2] - CODE_LANES), jnp.bfloat16),
        in_specs=[VMEM],
        out_specs=VMEM,
        compiler_params=pltpu.CompilerParams(vmem_limit_bytes=8 * 2**20),
    )(packet)


def on_device(
    phi_rows, psi_rows, stiffness, coord_fixed, coord_con, elem_zone, partner, owner_slot
):
    nf, nc = coord_fixed.shape[2], coord_con.shape[2]
    mine = coord_fixed.shape[1]
    modes = N_ROW * mine
    width = nc + nf + -(nc + nf) % 128

    sent = packets(coord_con[0], coord_fixed[0], N_ROW // 2, width)
    own = lax.all_to_all(sent, ("y", "zhi"), 0, 0, tiled=True).reshape(modes // 2, width)

    phi, codes = early(elem_zone, owner_slot, phi_rows.T, width - nc)
    own, phi, codes = lax.optimization_barrier((own, phi, codes))
    other = lax.ppermute(own, "core", [(0, 1), (1, 0)])

    psi = fetched(psi_rows)
    energy = block_energy(partner, own, other, phi, psi, stiffness, codes, N_FIRST)
    gathered = lax.all_to_all(energy, FIRST, 0, 0, tiled=True)
    partial_sums = zone_sums(gathered, 2 * N_SECOND).reshape(N_SECOND, 2, modes)
    received = lax.all_to_all(partial_sums, SECOND, 0, 0, tiled=True)
    return jnp.sum(received.astype(jnp.float32), axis=0)


def solution(mesh):
    fine = Mesh(mesh.devices.reshape(SIZES), AXES)
    sub, row = AXES[:2], AXES[2:]
    placed = (
        P(AXES, None),
        P(AXES, None),
        P(AXES, None, None),
        P(sub, row, None),
        P(sub, row, None),
        P(AXES),
        P(AXES),
        P(),
    )
    return jax.shard_map(
        on_device, mesh=fine, in_specs=placed, out_specs=P(AXES, None), check_vma=False
    )
```

```python
import jax
import jax.numpy as jnp
from jax import lax
from jax.experimental import pallas as pl
from jax.experimental.pallas import tpu as pltpu
from jax.sharding import Mesh, PartitionSpec as P

AXES = ("zlo", "x", "y", "zhi", "core")
SIZES = (4, 4, 8, 2, 2)
SIZE = dict(zip(AXES, SIZES))
SLOT_STEP = {"zlo": 256, "x": 64, "y": 8, "zhi": 4, "core": 2}
FIRST = ("x", "core")
SECOND = ("zlo", "y", "zhi")
N_FIRST = 8
N_SECOND = 64
N_ROW = 32
NT = (((1,), (1,)), ((), ()))
TN = (((0,), (0,)), ((), ()))
VMEM = pl.BlockSpec(memory_space=pltpu.VMEM)
SMEM = pl.BlockSpec(memory_space=pltpu.SMEM)
CODE_LANES = 128


def packet_kernel(con_ref, fixed_ref, out_ref):
    mine, nf = fixed_ref.shape
    nc = con_ref.shape[1]
    whole = nf // 128 * 128
    head = jnp.concatenate([con_ref[...], fixed_ref[:, :whole]], axis=1)
    blank = jnp.zeros((mine, out_ref.shape[2] - nc - nf), out_ref.dtype)
    tail = jnp.concatenate([fixed_ref[:, whole:], blank], axis=1)
    for i in range(out_ref.shape[0]):
        out_ref[i, :, : nc + whole] = head
        out_ref[i, :, nc + whole :] = tail


def packets(con, fixed, copies, width):
    return pl.pallas_call(
        packet_kernel,
        out_shape=jax.ShapeDtypeStruct((copies, con.shape[0], width), con.dtype),
        in_specs=[VMEM, VMEM],
        out_specs=VMEM,
        compiler_params=pltpu.CompilerParams(vmem_limit_bytes=56 * 2**20),
    )(con, fixed)


def early_kernel(elem_zone_ref, owner_slot_ref, phi_ref, rows_ref, codes_ref):
    nf, rows = phi_ref.shape
    rows_ref[:, :nf] = phi_ref[...].T
    rows_ref[:, nf:] = jnp.zeros((rows, rows_ref.shape[1] - nf), rows_ref.dtype)
    row = lax.broadcasted_iota(jnp.int32, codes_ref.shape, 0)
    lane = lax.broadcasted_iota(jnp.int32, codes_ref.shape, 1)
    codes = jnp.zeros(codes_ref.shape, jnp.int32)
    for b in range(codes_ref.shape[0]):
        slot = owner_slot_ref[elem_zone_ref[b]]
        codes = jnp.where((row == b) & (lane == 0), slot // 32, codes)
        codes = jnp.where((row == b) & (lane == 1), slot % 32, codes)
    codes_ref[...] = codes.astype(jnp.float32).astype(codes_ref.dtype)


def early(elem_zone, owner_slot, phi_t, width):
    return pl.pallas_call(
        early_kernel,
        out_shape=(
            jax.ShapeDtypeStruct((phi_t.shape[1], width), phi_t.dtype),
            jax.ShapeDtypeStruct((elem_zone.shape[0], CODE_LANES), jnp.bfloat16),
        ),
        in_specs=[SMEM, SMEM, VMEM],
        out_specs=(VMEM, VMEM),
        compiler_params=pltpu.CompilerParams(vmem_limit_bytes=16 * 2**20),
        cost_estimate=pl.CostEstimate(flops=0, bytes_accessed=8 * 2**20, transcendentals=0),
    )(elem_zone, owner_slot, phi_t)


def fetch_kernel(psi_ref, kept_ref, arrived):
    chunks = arrived.shape[0]
    step = psi_ref.shape[0] // chunks
    parts = [pl.ds(i * step, step) for i in range(chunks)]
    copies = [
        pltpu.make_async_copy(psi_ref.at[part], kept_ref.at[part], arrived.at[i])
        for i, part in enumerate(parts)
    ]
    for copy in copies:
        copy.start()
    for copy in copies:
        copy.wait()


def fetched(psi, chunks=4):
    return pl.pallas_call(
        fetch_kernel,
        out_shape=pltpu.VMEM(psi.shape, psi.dtype),
        in_specs=[pl.BlockSpec(memory_space=pltpu.HBM)],
        out_specs=VMEM,
        scratch_shapes=[pltpu.SemaphoreType.DMA((chunks,))],
        compiler_params=pltpu.CompilerParams(vmem_limit_bytes=57 * 2**20),
        cost_estimate=pl.CostEstimate(flops=0, bytes_accessed=6 * 2**20, transcendentals=0),
    )(psi)


def energy_kernel(
    partner_ref, own_ref, other_ref, phi_ref, psi_ref, stiffness_ref, codes_ref, out_ref, coords, shapes
):
    half = other_ref.shape[0]
    nc = psi_ref.shape[1]
    nblocks, block, _ = stiffness_ref.shape
    modes = 2 * half
    coords[:half] = own_ref[...]
    coords[half:] = other_ref[...]
    total = lax.dot_general(psi_ref[...], coords[:, :nc], NT, preferred_element_type=jnp.float32)
    total = total + lax.dot_general(
        phi_ref[...], coords[:, nc:], NT, preferred_element_type=jnp.float32
    )
    for b in range(nblocks):
        shapes[b] = total[b * block : (b + 1) * block].astype(shapes.dtype)
    sums = []
    for b in range(nblocks):
        own = shapes[b].astype(jnp.float32)
        partner = shapes[partner_ref[b]].astype(jnp.float32)
        relative = (own - partner).astype(jnp.bfloat16)
        pushed = jnp.dot(stiffness_ref[b], relative, preferred_element_type=jnp.float32)
        sums.append(jnp.sum(relative.astype(jnp.float32) * pushed, axis=0, keepdims=True))
    energy = jnp.concatenate(sums, axis=0).astype(jnp.bfloat16)
    source = lax.broadcasted_iota(jnp.int32, (modes, modes), 0)
    target = lax.broadcasted_iota(jnp.int32, (modes, modes), 1)
    core = (source // half + lax.axis_index("core")) % 2
    peer = (source % half) // 8
    ordered = peer % 8 * 32 + peer // 8 * 16 + core * 8 + source % 8
    move = (ordered == target).astype(jnp.float32).astype(jnp.bfloat16)
    energy = jnp.dot(energy, move, preferred_element_type=jnp.float32).astype(jnp.bfloat16)
    for i in range(out_ref.shape[0]):
        out_ref[i, :, :modes] = energy
        out_ref[i, :, modes:] = codes_ref[...]


def block_energy(partner, own, other, phi, psi, stiffness, codes, copies):
    nblocks, block, _ = stiffness.shape
    modes = 2 * other.shape[0]
    return pl.pallas_call(
        energy_kernel,
        out_shape=jax.ShapeDtypeStruct((copies, nblocks, modes + CODE_LANES), jnp.bfloat16),
        in_specs=[SMEM, VMEM, VMEM, VMEM, VMEM, VMEM, VMEM],
        out_specs=VMEM,
        scratch_shapes=[
            pltpu.VMEM((modes, own.shape[1]), jnp.bfloat16),
            pltpu.VMEM((nblocks, block, modes), jnp.bfloat16),
        ],
        compiler_params=pltpu.CompilerParams(vmem_limit_bytes=24 * 2**20),
        cost_estimate=pl.CostEstimate(flops=2**30, bytes_accessed=6 * 2**20, transcendentals=0),
    )(partner, own, other, phi, psi, stiffness, codes)


def zone_kernel(packet_ref, out_ref):
    peers, nblocks, width = packet_ref.shape
    modes = width - CODE_LANES
    packet = packet_ref[...].astype(jnp.float32).reshape(peers * nblocks, width)
    slot = packet[:, modes : modes + 1] * 32.0 + packet[:, modes + 1 : modes + 2]
    place = lax.broadcasted_iota(jnp.int32, (1, out_ref.shape[0]), 1)
    owned = place % 2 + sum(SLOT_STEP[axis] * lax.axis_index(axis) for axis in FIRST)
    peer = place // 2
    for axis in reversed(SECOND):
        owned = owned + peer % SIZE[axis] * SLOT_STEP[axis]
        peer = peer // SIZE[axis]
    chosen = (slot == owned.astype(jnp.float32)).astype(jnp.float32).astype(jnp.bfloat16)
    energy = packet[:, :modes].astype(jnp.bfloat16)
    sums = lax.dot_general(chosen, energy, TN, preferred_element_type=jnp.float32)
    out_ref[...] = sums.astype(out_ref.dtype)


def zone_sums(packet, slots):
    return pl.pallas_call(
        zone_kernel,
        out_shape=jax.ShapeDtypeStruct((slots, packet.shape[2] - CODE_LANES), jnp.bfloat16),
        in_specs=[VMEM],
        out_specs=VMEM,
        compiler_params=pltpu.CompilerParams(vmem_limit_bytes=8 * 2**20),
    )(packet)


def on_device(
    phi_rows, psi_rows, stiffness, coord_fixed, coord_con, elem_zone, partner, owner_slot
):
    nf, nc = coord_fixed.shape[2], coord_con.shape[2]
    mine = coord_fixed.shape[1]
    modes = N_ROW * mine
    width = nc + nf + -(nc + nf) % 128

    sent = packets(coord_con[0], coord_fixed[0], N_ROW // 2, width)
    own = lax.all_to_all(sent, ("zhi", "y"), 0, 0, tiled=True).reshape(modes // 2, width)

    phi, codes = early(elem_zone, owner_slot, phi_rows.T, width - nc)
    own, phi, codes = lax.optimization_barrier((own, phi, codes))
    other = lax.ppermute(own, "core", [(0, 1), (1, 0)])

    psi = fetched(psi_rows)
    energy = block_energy(partner, own, other, phi, psi, stiffness, codes, N_FIRST)
    gathered = lax.all_to_all(energy, FIRST, 0, 0, tiled=True)
    partial_sums = zone_sums(gathered, 2 * N_SECOND).reshape(N_SECOND, 2, modes)
    received = lax.all_to_all(partial_sums, SECOND, 0, 0, tiled=True)
    return jnp.sum(received.astype(jnp.float32), axis=0)


def solution(mesh):
    fine = Mesh(mesh.devices.reshape(SIZES), AXES)
    sub, row = AXES[:2], AXES[2:]
    placed = (
        P(AXES, None),
        P(AXES, None),
        P(AXES, None, None),
        P(sub, row, None),
        P(sub, row, None),
        P(AXES),
        P(AXES),
        P(),
    )
    return jax.shard_map(
        on_device, mesh=fine, in_specs=placed, out_specs=P(AXES, None), check_vma=False
    )
```

```python
import jax
import jax.numpy as jnp
from jax import lax
from jax.experimental import pallas as pl
from jax.experimental.pallas import tpu as pltpu
from jax.sharding import Mesh, PartitionSpec as P

AXES = ("zlo", "x", "y", "zhi", "core")
SIZES = (4, 4, 8, 2, 2)
SIZE = dict(zip(AXES, SIZES))
SLOT_STEP = {"zlo": 256, "x": 64, "y": 8, "zhi": 4, "core": 2}
FIRST = ("x", "core")
SECOND = ("zlo", "y", "zhi")
N_FIRST = 8
N_SECOND = 64
N_ROW = 32
NT = (((1,), (1,)), ((), ()))
TN = (((0,), (0,)), ((), ()))
VMEM = pl.BlockSpec(memory_space=pltpu.VMEM)
SMEM = pl.BlockSpec(memory_space=pltpu.SMEM)
CODE_LANES = 128


def packet_kernel(con_ref, fixed_ref, out_ref):
    mine, nf = fixed_ref.shape
    nc = con_ref.shape[1]
    whole = nf // 128 * 128
    head = jnp.concatenate([con_ref[...], fixed_ref[:, :whole]], axis=1)
    blank = jnp.zeros((mine, out_ref.shape[2] - nc - nf), out_ref.dtype)
    tail = jnp.concatenate([fixed_ref[:, whole:], blank], axis=1)
    for i in range(out_ref.shape[0]):
        out_ref[i, :, : nc + whole] = head
        out_ref[i, :, nc + whole :] = tail


def packets(con, fixed, copies, width):
    return pl.pallas_call(
        packet_kernel,
        out_shape=jax.ShapeDtypeStruct((copies, con.shape[0], width), con.dtype),
        in_specs=[VMEM, VMEM],
        out_specs=VMEM,
        compiler_params=pltpu.CompilerParams(vmem_limit_bytes=56 * 2**20),
    )(con, fixed)


def early_kernel(elem_zone_ref, owner_slot_ref, phi_ref, rows_ref, codes_ref):
    nf, rows = phi_ref.shape
    rows_ref[:, :nf] = phi_ref[...].T
    rows_ref[:, nf:] = jnp.zeros((rows, rows_ref.shape[1] - nf), rows_ref.dtype)
    row = lax.broadcasted_iota(jnp.int32, codes_ref.shape, 0)
    lane = lax.broadcasted_iota(jnp.int32, codes_ref.shape, 1)
    codes = jnp.zeros(codes_ref.shape, jnp.int32)
    for b in range(codes_ref.shape[0]):
        slot = owner_slot_ref[elem_zone_ref[b]]
        codes = jnp.where((row == b) & (lane == 0), slot // 32, codes)
        codes = jnp.where((row == b) & (lane == 1), slot % 32, codes)
    codes_ref[...] = codes.astype(jnp.float32).astype(codes_ref.dtype)


def early(elem_zone, owner_slot, phi_t, width):
    return pl.pallas_call(
        early_kernel,
        out_shape=(
            jax.ShapeDtypeStruct((phi_t.shape[1], width), phi_t.dtype),
            jax.ShapeDtypeStruct((elem_zone.shape[0], CODE_LANES), jnp.bfloat16),
        ),
        in_specs=[SMEM, SMEM, VMEM],
        out_specs=(VMEM, VMEM),
        compiler_params=pltpu.CompilerParams(vmem_limit_bytes=16 * 2**20),
        cost_estimate=pl.CostEstimate(flops=0, bytes_accessed=8 * 2**20, transcendentals=0),
    )(elem_zone, owner_slot, phi_t)


def fetch_kernel(psi_ref, kept_ref, arrived):
    chunks = arrived.shape[0]
    step = psi_ref.shape[0] // chunks
    parts = [pl.ds(i * step, step) for i in range(chunks)]
    copies = [
        pltpu.make_async_copy(psi_ref.at[part], kept_ref.at[part], arrived.at[i])
        for i, part in enumerate(parts)
    ]
    for copy in copies:
        copy.start()
    for copy in copies:
        copy.wait()


def fetched(psi, chunks=4):
    return pl.pallas_call(
        fetch_kernel,
        out_shape=pltpu.VMEM(psi.shape, psi.dtype),
        in_specs=[pl.BlockSpec(memory_space=pltpu.HBM)],
        out_specs=VMEM,
        scratch_shapes=[pltpu.SemaphoreType.DMA((chunks,))],
        compiler_params=pltpu.CompilerParams(vmem_limit_bytes=57 * 2**20),
        cost_estimate=pl.CostEstimate(flops=0, bytes_accessed=6 * 2**20, transcendentals=0),
    )(psi)


def energy_kernel(
    partner_ref, own_ref, other_ref, phi_ref, psi_ref, stiffness_ref, codes_ref, out_ref, coords, shapes
):
    half = other_ref.shape[0]
    nc = psi_ref.shape[1]
    nblocks, block, _ = stiffness_ref.shape
    modes = 2 * half
    coords[:half] = own_ref[...]
    coords[half:] = other_ref[...]
    total = lax.dot_general(psi_ref[...], coords[:, :nc], NT, preferred_element_type=jnp.float32)
    total = total + lax.dot_general(
        phi_ref[...], coords[:, nc:], NT, preferred_element_type=jnp.float32
    )
    for b in range(nblocks):
        shapes[b] = total[b * block : (b + 1) * block].astype(shapes.dtype)
    sums = []
    for b in range(nblocks):
        own = shapes[b].astype(jnp.float32)
        partner = shapes[partner_ref[b]].astype(jnp.float32)
        relative = (own - partner).astype(jnp.bfloat16)
        pushed = jnp.dot(stiffness_ref[b], relative, preferred_element_type=jnp.float32)
        sums.append(jnp.sum(relative.astype(jnp.float32) * pushed, axis=0, keepdims=True))
    energy = jnp.concatenate(sums, axis=0).astype(jnp.bfloat16)
    source = lax.broadcasted_iota(jnp.int32, (modes, modes), 0)
    target = lax.broadcasted_iota(jnp.int32, (modes, modes), 1)
    core = (source // half + lax.axis_index("core")) % 2
    peer = half // 8 - 1 - (source % half) // 8
    ordered = peer % 8 * 32 + peer // 8 * 16 + core * 8 + source % 8
    move = (ordered == target).astype(jnp.float32).astype(jnp.bfloat16)
    energy = jnp.dot(energy, move, preferred_element_type=jnp.float32).astype(jnp.bfloat16)
    for i in range(out_ref.shape[0]):
        out_ref[i, :, :modes] = energy
        out_ref[i, :, modes:] = codes_ref[...]


def block_energy(partner, own, other, phi, psi, stiffness, codes, copies):
    nblocks, block, _ = stiffness.shape
    modes = 2 * other.shape[0]
    return pl.pallas_call(
        energy_kernel,
        out_shape=jax.ShapeDtypeStruct((copies, nblocks, modes + CODE_LANES), jnp.bfloat16),
        in_specs=[SMEM, VMEM, VMEM, VMEM, VMEM, VMEM, VMEM],
        out_specs=VMEM,
        scratch_shapes=[
            pltpu.VMEM((modes, own.shape[1]), jnp.bfloat16),
            pltpu.VMEM((nblocks, block, modes), jnp.bfloat16),
        ],
        compiler_params=pltpu.CompilerParams(vmem_limit_bytes=24 * 2**20),
        cost_estimate=pl.CostEstimate(flops=2**30, bytes_accessed=6 * 2**20, transcendentals=0),
    )(partner, own, other, phi, psi, stiffness, codes)


def zone_kernel(packet_ref, out_ref):
    peers, nblocks, width = packet_ref.shape
    modes = width - CODE_LANES
    packet = packet_ref[...].astype(jnp.float32).reshape(peers * nblocks, width)
    slot = packet[:, modes : modes + 1] * 32.0 + packet[:, modes + 1 : modes + 2]
    place = lax.broadcasted_iota(jnp.int32, (1, out_ref.shape[0]), 1)
    owned = place % 2 + sum(SLOT_STEP[axis] * lax.axis_index(axis) for axis in FIRST)
    peer = N_SECOND - 1 - place // 2
    for axis in reversed(SECOND):
        owned = owned + peer % SIZE[axis] * SLOT_STEP[axis]
        peer = peer // SIZE[axis]
    chosen = (slot == owned.astype(jnp.float32)).astype(jnp.float32).astype(jnp.bfloat16)
    energy = packet[:, :modes].astype(jnp.bfloat16)
    sums = lax.dot_general(chosen, energy, TN, preferred_element_type=jnp.float32)
    out_ref[...] = sums.astype(out_ref.dtype)


def zone_sums(packet, slots):
    return pl.pallas_call(
        zone_kernel,
        out_shape=jax.ShapeDtypeStruct((slots, packet.shape[2] - CODE_LANES), jnp.bfloat16),
        in_specs=[VMEM],
        out_specs=VMEM,
        compiler_params=pltpu.CompilerParams(vmem_limit_bytes=8 * 2**20),
    )(packet)


def exchange(blocks, axes):
    members = list(range(blocks.shape[0]))[::-1]
    return lax.all_to_all(blocks, axes, 0, 0, axis_index_groups=[members], tiled=True)


def on_device(
    phi_rows, psi_rows, stiffness, coord_fixed, coord_con, elem_zone, partner, owner_slot
):
    nf, nc = coord_fixed.shape[2], coord_con.shape[2]
    mine = coord_fixed.shape[1]
    modes = N_ROW * mine
    width = nc + nf + -(nc + nf) % 128

    sent = packets(coord_con[0], coord_fixed[0], N_ROW // 2, width)
    own = exchange(sent, ("zhi", "y")).reshape(modes // 2, width)

    phi, codes = early(elem_zone, owner_slot, phi_rows.T, width - nc)
    own, phi, codes = lax.optimization_barrier((own, phi, codes))
    other = lax.ppermute(own, "core", [(0, 1), (1, 0)])

    psi = fetched(psi_rows)
    energy = block_energy(partner, own, other, phi, psi, stiffness, codes, N_FIRST)
    gathered = exchange(energy, FIRST)
    partial_sums = zone_sums(gathered, 2 * N_SECOND).reshape(N_SECOND, 2, modes)
    received = exchange(partial_sums, SECOND)
    return jnp.sum(received.astype(jnp.float32), axis=0)


def solution(mesh):
    fine = Mesh(mesh.devices.reshape(SIZES), AXES)
    sub, row = AXES[:2], AXES[2:]
    placed = (
        P(AXES, None),
        P(AXES, None),
        P(AXES, None, None),
        P(sub, row, None),
        P(sub, row, None),
        P(AXES),
        P(AXES),
        P(),
    )
    return jax.shard_map(
        on_device, mesh=fine, in_specs=placed, out_specs=P(AXES, None), check_vma=False
    )
```

```python
import jax
import jax.numpy as jnp
from jax import lax
from jax.experimental import pallas as pl
from jax.experimental.pallas import tpu as pltpu
from jax.sharding import Mesh, PartitionSpec as P

AXES = ("zlo", "x", "y", "zhi", "core")
SIZES = (4, 4, 8, 2, 2)
SIZE = dict(zip(AXES, SIZES))
SLOT_STEP = {"zlo": 256, "x": 64, "y": 8, "zhi": 4, "core": 2}
FIRST = ("x", "core")
SECOND = ("y", "zhi", "zlo")
N_FIRST = 8
N_SECOND = 64
N_ROW = 32
GATHER_ORDER = [8 * zhi + 4 * y2 + 2 * y1 + y0 for zhi in (0, 1) for y1 in (0, 1) for y2 in (0, 1) for y0 in (0, 1)]
NT = (((1,), (1,)), ((), ()))
TN = (((0,), (0,)), ((), ()))
VMEM = pl.BlockSpec(memory_space=pltpu.VMEM)
SMEM = pl.BlockSpec(memory_space=pltpu.SMEM)
CODE_LANES = 128


def packet_kernel(con_ref, fixed_ref, out_ref):
    mine, nf = fixed_ref.shape
    nc = con_ref.shape[1]
    whole = nf // 128 * 128
    head = jnp.concatenate([con_ref[...], fixed_ref[:, :whole]], axis=1)
    blank = jnp.zeros((mine, out_ref.shape[2] - nc - nf), out_ref.dtype)
    tail = jnp.concatenate([fixed_ref[:, whole:], blank], axis=1)
    for i in range(out_ref.shape[0]):
        out_ref[i, :, : nc + whole] = head
        out_ref[i, :, nc + whole :] = tail


def packets(con, fixed, copies, width):
    return pl.pallas_call(
        packet_kernel,
        out_shape=jax.ShapeDtypeStruct((copies, con.shape[0], width), con.dtype),
        in_specs=[VMEM, VMEM],
        out_specs=VMEM,
        compiler_params=pltpu.CompilerParams(vmem_limit_bytes=56 * 2**20),
    )(con, fixed)


def early_kernel(elem_zone_ref, owner_slot_ref, phi_ref, rows_ref, codes_ref):
    nf, rows = phi_ref.shape
    rows_ref[:, :nf] = phi_ref[...].T
    rows_ref[:, nf:] = jnp.zeros((rows, rows_ref.shape[1] - nf), rows_ref.dtype)
    row = lax.broadcasted_iota(jnp.int32, codes_ref.shape, 0)
    lane = lax.broadcasted_iota(jnp.int32, codes_ref.shape, 1)
    codes = jnp.zeros(codes_ref.shape, jnp.int32)
    for b in range(codes_ref.shape[0]):
        slot = owner_slot_ref[elem_zone_ref[b]]
        codes = jnp.where((row == b) & (lane == 0), slot // 32, codes)
        codes = jnp.where((row == b) & (lane == 1), slot % 32, codes)
    codes_ref[...] = codes.astype(jnp.float32).astype(codes_ref.dtype)


def early(elem_zone, owner_slot, phi_t, width):
    return pl.pallas_call(
        early_kernel,
        out_shape=(
            jax.ShapeDtypeStruct((phi_t.shape[1], width), phi_t.dtype),
            jax.ShapeDtypeStruct((elem_zone.shape[0], CODE_LANES), jnp.bfloat16),
        ),
        in_specs=[SMEM, SMEM, VMEM],
        out_specs=(VMEM, VMEM),
        compiler_params=pltpu.CompilerParams(vmem_limit_bytes=16 * 2**20),
        cost_estimate=pl.CostEstimate(flops=0, bytes_accessed=8 * 2**20, transcendentals=0),
    )(elem_zone, owner_slot, phi_t)


def fetch_kernel(psi_ref, kept_ref, arrived):
    chunks = arrived.shape[0]
    step = psi_ref.shape[0] // chunks
    parts = [pl.ds(i * step, step) for i in range(chunks)]
    copies = [
        pltpu.make_async_copy(psi_ref.at[part], kept_ref.at[part], arrived.at[i])
        for i, part in enumerate(parts)
    ]
    for copy in copies:
        copy.start()
    for copy in copies:
        copy.wait()


def fetched(psi, chunks=4):
    return pl.pallas_call(
        fetch_kernel,
        out_shape=pltpu.VMEM(psi.shape, psi.dtype),
        in_specs=[pl.BlockSpec(memory_space=pltpu.HBM)],
        out_specs=VMEM,
        scratch_shapes=[pltpu.SemaphoreType.DMA((chunks,))],
        compiler_params=pltpu.CompilerParams(vmem_limit_bytes=57 * 2**20),
        cost_estimate=pl.CostEstimate(flops=0, bytes_accessed=6 * 2**20, transcendentals=0),
    )(psi)


def energy_kernel(
    partner_ref, own_ref, other_ref, phi_ref, psi_ref, stiffness_ref, codes_ref, out_ref, coords, shapes
):
    half = other_ref.shape[0]
    nc = psi_ref.shape[1]
    nblocks, block, _ = stiffness_ref.shape
    modes = 2 * half
    coords[:half] = own_ref[...]
    coords[half:] = other_ref[...]
    total = lax.dot_general(psi_ref[...], coords[:, :nc], NT, preferred_element_type=jnp.float32)
    total = total + lax.dot_general(
        phi_ref[...], coords[:, nc:], NT, preferred_element_type=jnp.float32
    )
    for b in range(nblocks):
        shapes[b] = total[b * block : (b + 1) * block].astype(shapes.dtype)
    sums = []
    for b in range(nblocks):
        own = shapes[b].astype(jnp.float32)
        partner = shapes[partner_ref[b]].astype(jnp.float32)
        relative = (own - partner).astype(jnp.bfloat16)
        pushed = jnp.dot(stiffness_ref[b], relative, preferred_element_type=jnp.float32)
        sums.append(jnp.sum(relative.astype(jnp.float32) * pushed, axis=0, keepdims=True))
    energy = jnp.concatenate(sums, axis=0).astype(jnp.bfloat16)
    source = lax.broadcasted_iota(jnp.int32, (modes, modes), 0)
    target = lax.broadcasted_iota(jnp.int32, (modes, modes), 1)
    core = (source // half + lax.axis_index("core")) % 2
    peer = half // 8 - 1 - (source % half) // 8
    y = peer % 2 + peer // 4 % 2 * 2 + peer // 2 % 2 * 4
    ordered = y * 32 + peer // 8 * 16 + core * 8 + source % 8
    move = (ordered == target).astype(jnp.float32).astype(jnp.bfloat16)
    energy = jnp.dot(energy, move, preferred_element_type=jnp.float32).astype(jnp.bfloat16)
    for i in range(out_ref.shape[0]):
        out_ref[i, :, :modes] = energy
        out_ref[i, :, modes:] = codes_ref[...]


def block_energy(partner, own, other, phi, psi, stiffness, codes, copies):
    nblocks, block, _ = stiffness.shape
    modes = 2 * other.shape[0]
    return pl.pallas_call(
        energy_kernel,
        out_shape=jax.ShapeDtypeStruct((copies, nblocks, modes + CODE_LANES), jnp.bfloat16),
        in_specs=[SMEM, VMEM, VMEM, VMEM, VMEM, VMEM, VMEM],
        out_specs=VMEM,
        scratch_shapes=[
            pltpu.VMEM((modes, own.shape[1]), jnp.bfloat16),
            pltpu.VMEM((nblocks, block, modes), jnp.bfloat16),
        ],
        compiler_params=pltpu.CompilerParams(vmem_limit_bytes=24 * 2**20),
        cost_estimate=pl.CostEstimate(flops=2**30, bytes_accessed=6 * 2**20, transcendentals=0),
    )(partner, own, other, phi, psi, stiffness, codes)


def zone_kernel(packet_ref, out_ref):
    peers, nblocks, width = packet_ref.shape
    modes = width - CODE_LANES
    packet = packet_ref[...].astype(jnp.float32).reshape(peers * nblocks, width)
    slot = packet[:, modes : modes + 1] * 32.0 + packet[:, modes + 1 : modes + 2]
    place = lax.broadcasted_iota(jnp.int32, (1, out_ref.shape[0]), 1)
    owned = place % 2 + sum(SLOT_STEP[axis] * lax.axis_index(axis) for axis in FIRST)
    peer = N_SECOND - 1 - place // 2
    for axis in reversed(SECOND):
        owned = owned + peer % SIZE[axis] * SLOT_STEP[axis]
        peer = peer // SIZE[axis]
    chosen = (slot == owned.astype(jnp.float32)).astype(jnp.float32).astype(jnp.bfloat16)
    energy = packet[:, :modes].astype(jnp.bfloat16)
    sums = lax.dot_general(chosen, energy, TN, preferred_element_type=jnp.float32)
    out_ref[...] = sums.astype(out_ref.dtype)


def zone_sums(packet, slots):
    return pl.pallas_call(
        zone_kernel,
        out_shape=jax.ShapeDtypeStruct((slots, packet.shape[2] - CODE_LANES), jnp.bfloat16),
        in_specs=[VMEM],
        out_specs=VMEM,
        compiler_params=pltpu.CompilerParams(vmem_limit_bytes=8 * 2**20),
    )(packet)


def exchange(blocks, axes, order=None):
    members = list(order or range(blocks.shape[0]))[::-1]
    return lax.all_to_all(blocks, axes, 0, 0, axis_index_groups=[members], tiled=True)


def on_device(
    phi_rows, psi_rows, stiffness, coord_fixed, coord_con, elem_zone, partner, owner_slot
):
    nf, nc = coord_fixed.shape[2], coord_con.shape[2]
    mine = coord_fixed.shape[1]
    modes = N_ROW * mine
    width = nc + nf + -(nc + nf) % 128

    sent = packets(coord_con[0], coord_fixed[0], N_ROW // 2, width)
    own = exchange(sent, ("zhi", "y"), GATHER_ORDER).reshape(modes // 2, width)

    phi, codes = early(elem_zone, owner_slot, phi_rows.T, width - nc)
    own, phi, codes = lax.optimization_barrier((own, phi, codes))
    other = lax.ppermute(own, "core", [(0, 1), (1, 0)])

    psi = fetched(psi_rows)
    energy = block_energy(partner, own, other, phi, psi, stiffness, codes, N_FIRST)
    gathered = exchange(energy, FIRST)
    partial_sums = zone_sums(gathered, 2 * N_SECOND).reshape(N_SECOND, 2, modes)
    received = exchange(partial_sums, SECOND)
    return jnp.sum(received.astype(jnp.float32), axis=0)


def solution(mesh):
    fine = Mesh(mesh.devices.reshape(SIZES), AXES)
    sub, row = AXES[:2], AXES[2:]
    placed = (
        P(AXES, None),
        P(AXES, None),
        P(AXES, None, None),
        P(sub, row, None),
        P(sub, row, None),
        P(AXES),
        P(AXES),
        P(),
    )
    return jax.shard_map(
        on_device, mesh=fine, in_specs=placed, out_specs=P(AXES, None), check_vma=False
    )
```

```python
import jax
import jax.numpy as jnp
from jax import lax
from jax.experimental import pallas as pl
from jax.experimental.pallas import tpu as pltpu
from jax.sharding import Mesh, PartitionSpec as P

AXES = ("zlo", "x", "y", "zhi", "core")
SIZES = (4, 4, 8, 2, 2)
SIZE = dict(zip(AXES, SIZES))
SLOT_STEP = {"zlo": 256, "x": 64, "y": 8, "zhi": 4, "core": 2}
FIRST = ("x", "core")
SECOND = ("zlo", "y", "zhi")
N_FIRST = 8
N_SECOND = 64
N_ROW = 32
NT = (((1,), (1,)), ((), ()))
TN = (((0,), (0,)), ((), ()))
VMEM = pl.BlockSpec(memory_space=pltpu.VMEM)
SMEM = pl.BlockSpec(memory_space=pltpu.SMEM)
CODE_LANES = 128


def packet_kernel(con_ref, fixed_ref, out_ref):
    mine, nf = fixed_ref.shape
    nc = con_ref.shape[1]
    whole = nf // 128 * 128
    head = jnp.concatenate([con_ref[...], fixed_ref[:, :whole]], axis=1)
    blank = jnp.zeros((mine, out_ref.shape[2] - nc - nf), out_ref.dtype)
    tail = jnp.concatenate([fixed_ref[:, whole:], blank], axis=1)
    for i in range(out_ref.shape[0]):
        out_ref[i, :, : nc + whole] = head
        out_ref[i, :, nc + whole :] = tail


def packets(con, fixed, copies, width):
    return pl.pallas_call(
        packet_kernel,
        out_shape=jax.ShapeDtypeStruct((copies, con.shape[0], width), con.dtype),
        in_specs=[VMEM, VMEM],
        out_specs=VMEM,
        compiler_params=pltpu.CompilerParams(vmem_limit_bytes=56 * 2**20),
    )(con, fixed)


def early_kernel(elem_zone_ref, owner_slot_ref, phi_ref, rows_ref, codes_ref, move_ref):
    nf, rows = phi_ref.shape
    rows_ref[:, :nf] = phi_ref[...].T
    rows_ref[:, nf:] = jnp.zeros((rows, rows_ref.shape[1] - nf), rows_ref.dtype)
    row = lax.broadcasted_iota(jnp.int32, codes_ref.shape, 0)
    lane = lax.broadcasted_iota(jnp.int32, codes_ref.shape, 1)
    codes = jnp.zeros(codes_ref.shape, jnp.int32)
    for b in range(codes_ref.shape[0]):
        slot = owner_slot_ref[elem_zone_ref[b]]
        codes = jnp.where((row == b) & (lane == 0), slot // 32, codes)
        codes = jnp.where((row == b) & (lane == 1), slot % 32, codes)
    codes_ref[...] = codes.astype(jnp.float32).astype(codes_ref.dtype)
    modes = move_ref.shape[0]
    half = modes // 2
    source = lax.broadcasted_iota(jnp.int32, (modes, modes), 0)
    target = lax.broadcasted_iota(jnp.int32, (modes, modes), 1)
    core = (source // half + lax.axis_index("core")) % 2
    peer = half // 8 - 1 - (source % half) // 8
    ordered = peer % 8 * 32 + peer // 8 * 16 + core * 8 + source % 8
    move = (ordered == target).astype(jnp.float32).astype(jnp.bfloat16)
    move_ref[...] = move


def early(elem_zone, owner_slot, phi_t, width, modes):
    return pl.pallas_call(
        early_kernel,
        out_shape=(
            jax.ShapeDtypeStruct((phi_t.shape[1], width), phi_t.dtype),
            jax.ShapeDtypeStruct((elem_zone.shape[0], CODE_LANES), jnp.bfloat16),
            jax.ShapeDtypeStruct((modes, modes), jnp.bfloat16),
        ),
        in_specs=[SMEM, SMEM, VMEM],
        out_specs=(VMEM, VMEM, VMEM),
        compiler_params=pltpu.CompilerParams(vmem_limit_bytes=16 * 2**20),
        cost_estimate=pl.CostEstimate(flops=0, bytes_accessed=8 * 2**20, transcendentals=0),
    )(elem_zone, owner_slot, phi_t)


def fetch_kernel(psi_ref, kept_ref, arrived):
    chunks = arrived.shape[0]
    step = psi_ref.shape[0] // chunks
    parts = [pl.ds(i * step, step) for i in range(chunks)]
    copies = [
        pltpu.make_async_copy(psi_ref.at[part], kept_ref.at[part], arrived.at[i])
        for i, part in enumerate(parts)
    ]
    for copy in copies:
        copy.start()
    for copy in copies:
        copy.wait()


def fetched(psi, chunks=4):
    return pl.pallas_call(
        fetch_kernel,
        out_shape=pltpu.VMEM(psi.shape, psi.dtype),
        in_specs=[pl.BlockSpec(memory_space=pltpu.HBM)],
        out_specs=VMEM,
        scratch_shapes=[pltpu.SemaphoreType.DMA((chunks,))],
        compiler_params=pltpu.CompilerParams(vmem_limit_bytes=57 * 2**20),
        cost_estimate=pl.CostEstimate(flops=0, bytes_accessed=6 * 2**20, transcendentals=0),
    )(psi)


def energy_kernel(
    partner_ref, own_ref, other_ref, phi_ref, psi_ref, stiffness_ref, codes_ref, move_ref, out_ref, coords, shapes
):
    half = other_ref.shape[0]
    nc = psi_ref.shape[1]
    nblocks, block, _ = stiffness_ref.shape
    modes = 2 * half
    coords[:half] = own_ref[...]
    coords[half:] = other_ref[...]
    total = lax.dot_general(psi_ref[...], coords[:, :nc], NT, preferred_element_type=jnp.float32)
    total = total + lax.dot_general(
        phi_ref[...], coords[:, nc:], NT, preferred_element_type=jnp.float32
    )
    for b in range(nblocks):
        shapes[b] = total[b * block : (b + 1) * block].astype(shapes.dtype)
    sums = []
    for b in range(nblocks):
        own = shapes[b].astype(jnp.float32)
        partner = shapes[partner_ref[b]].astype(jnp.float32)
        relative = (own - partner).astype(jnp.bfloat16)
        pushed = jnp.dot(stiffness_ref[b], relative, preferred_element_type=jnp.float32)
        sums.append(jnp.sum(relative.astype(jnp.float32) * pushed, axis=0, keepdims=True))
    energy = jnp.concatenate(sums, axis=0).astype(jnp.bfloat16)
    energy = jnp.dot(energy, move_ref[...], preferred_element_type=jnp.float32).astype(jnp.bfloat16)
    for i in range(out_ref.shape[0]):
        out_ref[i, :, :modes] = energy
        out_ref[i, :, modes:] = codes_ref[...]


def block_energy(partner, own, other, phi, psi, stiffness, codes, move, copies):
    nblocks, block, _ = stiffness.shape
    modes = 2 * other.shape[0]
    return pl.pallas_call(
        energy_kernel,
        out_shape=jax.ShapeDtypeStruct((copies, nblocks, modes + CODE_LANES), jnp.bfloat16),
        in_specs=[SMEM, VMEM, VMEM, VMEM, VMEM, VMEM, VMEM, VMEM],
        out_specs=VMEM,
        scratch_shapes=[
            pltpu.VMEM((modes, own.shape[1]), jnp.bfloat16),
            pltpu.VMEM((nblocks, block, modes), jnp.bfloat16),
        ],
        compiler_params=pltpu.CompilerParams(vmem_limit_bytes=24 * 2**20),
        cost_estimate=pl.CostEstimate(flops=2**30, bytes_accessed=6 * 2**20, transcendentals=0),
    )(partner, own, other, phi, psi, stiffness, codes, move)


def zone_kernel(packet_ref, out_ref):
    peers, nblocks, width = packet_ref.shape
    modes = width - CODE_LANES
    packet = packet_ref[...].astype(jnp.float32).reshape(peers * nblocks, width)
    slot = packet[:, modes : modes + 1] * 32.0 + packet[:, modes + 1 : modes + 2]
    place = lax.broadcasted_iota(jnp.int32, (1, out_ref.shape[0]), 1)
    owned = place % 2 + sum(SLOT_STEP[axis] * lax.axis_index(axis) for axis in FIRST)
    peer = N_SECOND - 1 - place // 2
    for axis in reversed(SECOND):
        owned = owned + peer % SIZE[axis] * SLOT_STEP[axis]
        peer = peer // SIZE[axis]
    chosen = (slot == owned.astype(jnp.float32)).astype(jnp.float32).astype(jnp.bfloat16)
    energy = packet[:, :modes].astype(jnp.bfloat16)
    sums = lax.dot_general(chosen, energy, TN, preferred_element_type=jnp.float32)
    out_ref[...] = sums.astype(out_ref.dtype)


def zone_sums(packet, slots):
    return pl.pallas_call(
        zone_kernel,
        out_shape=jax.ShapeDtypeStruct((slots, packet.shape[2] - CODE_LANES), jnp.bfloat16),
        in_specs=[VMEM],
        out_specs=VMEM,
        compiler_params=pltpu.CompilerParams(vmem_limit_bytes=8 * 2**20),
    )(packet)


def exchange(blocks, axes):
    members = list(range(blocks.shape[0]))[::-1]
    return lax.all_to_all(blocks, axes, 0, 0, axis_index_groups=[members], tiled=True)


def on_device(
    phi_rows, psi_rows, stiffness, coord_fixed, coord_con, elem_zone, partner, owner_slot
):
    nf, nc = coord_fixed.shape[2], coord_con.shape[2]
    mine = coord_fixed.shape[1]
    modes = N_ROW * mine
    width = nc + nf + -(nc + nf) % 128

    sent = packets(coord_con[0], coord_fixed[0], N_ROW // 2, width)
    own = exchange(sent, ("zhi", "y")).reshape(modes // 2, width)

    phi, codes, move = early(elem_zone, owner_slot, phi_rows.T, width - nc, modes)
    own, phi, codes, move = lax.optimization_barrier((own, phi, codes, move))
    other = lax.ppermute(own, "core", [(0, 1), (1, 0)])

    psi = fetched(psi_rows)
    energy = block_energy(partner, own, other, phi, psi, stiffness, codes, move, N_FIRST)
    gathered = exchange(energy, FIRST)
    partial_sums = zone_sums(gathered, 2 * N_SECOND).reshape(N_SECOND, 2, modes)
    received = exchange(partial_sums, SECOND)
    return jnp.sum(received.astype(jnp.float32), axis=0)


def solution(mesh):
    fine = Mesh(mesh.devices.reshape(SIZES), AXES)
    sub, row = AXES[:2], AXES[2:]
    placed = (
        P(AXES, None),
        P(AXES, None),
        P(AXES, None, None),
        P(sub, row, None),
        P(sub, row, None),
        P(AXES),
        P(AXES),
        P(),
    )
    return jax.shard_map(
        on_device, mesh=fine, in_specs=placed, out_specs=P(AXES, None), check_vma=False
    )
```
